256 devices in a mesh: gx: 8 (over x, z_lo), gy: 32 (over y, z_hi, core).
Axes of the slice: x: 4, y: 4, z: 8 (z_hi: 4, z_lo: 2; z = z_hi * 2 + z_lo), core: 2. Of those that a mesh axis runs over, the one named last changes fastest.
Arguments:
- embeddings: bfloat16 [262144, 1024], P(('gx', 'gy')), may hold values from -7 to 7
Outputs:
- log_density: float32 [262144], P(('gx', 'gy'))
The draws below stay inside these ranges and needn't reach their ends.
All inputs are finite; a program needn't handle non-finite values.
Results may differ from the reference program's by a relative error of at most 0.0003.
Values may be sent and summed in bfloat16 or wider, within the bound.
No kernel may reach another device: no remote copies, remote signals or barrier semaphores. Data moves between devices by JAX's collectives and lax.ppermute only.
A program may use at most 64 MiB of HBM per device.

```python
import jax
import jax.numpy as jnp
from jax import lax

D = 1024
ROWS = 1024
ROUNDS = 4
BAND = 64
DOCS = 262144
N_GX = 8
N_GY = 32


def draw_embeddings(key, part):
    keys = jax.random.split(key, 10)
    doc_index = jnp.arange(DOCS, dtype=jnp.int32)
    doc_block = doc_index // ROWS
    block_x = doc_block // N_GY
    block_y = doc_block % N_GY
    doc_slot = jax.random.randint(keys[0], (DOCS,), 0, ROWS, dtype=jnp.int32)
    second_slot = jax.random.randint(keys[8], (DOCS,), 0, ROWS, dtype=jnp.int32)
    offset_x = jax.random.randint(keys[1], (ROWS,), 0, 2, dtype=jnp.int32)[doc_slot]
    offset_y = jax.random.randint(keys[2], (ROWS,), 0, 6, dtype=jnp.int32)[doc_slot]
    groups_x = (N_GX + 1) // 2
    groups_y = (N_GY + 5) // 6
    group_x = (block_x + offset_x) % N_GX // 2
    group_y = (block_y + offset_y) % N_GY // 6
    group = group_x * groups_y + group_y
    cluster = (group * ROWS + doc_slot).astype(jnp.int32)
    second = (group * ROWS + second_slot).astype(jnp.int32)
    clusters_all = groups_x * groups_y * ROWS
    centers = jnp.clip(jax.random.normal(keys[3], (clusters_all, D), jnp.float32), -3.2, 3.2)
    mixing = jax.random.uniform(keys[9], (DOCS,), jnp.float32, 0.0, 0.6)
    levels = jnp.exp(jax.random.uniform(keys[4], (clusters_all,), jnp.float32, jnp.log(1.0), jnp.log(1.4)))
    spreads = jnp.exp(jax.random.uniform(keys[5], (DOCS,), jnp.float32, jnp.log(0.12), jnp.log(0.4)))
    noise = jnp.clip(jax.random.normal(keys[6], (DOCS, D), jnp.float32), -4.0, 4.0)
    blended = (1.0 - mixing)[:, None] * centers[cluster] + mixing[:, None] * centers[second]
    values = levels[cluster][:, None] * blended + spreads[:, None] * noise
    return values.astype(jnp.bfloat16)


def setup_inputs(seed: int = 0) -> dict:
    streams_of = jax.random.split(jax.random.key(seed), 2)
    embeddings = draw_embeddings(jax.random.fold_in(streams_of[1], 71), 0)
    return dict(embeddings=embeddings)


def half_norms(block):
    values = block.astype(jnp.float32)
    return jnp.sum(values * values, axis=1) / (2.0 * BAND)


def kernel_block(left, left_half, right, right_half):
    inner = jnp.dot(left, right.T, preferred_element_type=jnp.float32)
    return jnp.exp(inner / BAND - left_half[:, None] - right_half[None, :])


def reference(embeddings):
    count = N_GX * N_GY
    shards = embeddings.reshape(count, ROWS, D)
    halves = half_norms(embeddings).reshape(count, ROWS)
    diagonal = lax.broadcasted_iota(jnp.int32, (ROWS, ROWS), 0) == lax.broadcasted_iota(jnp.int32, (ROWS, ROWS), 1)

    def per_device(index, totals):
        index = index.astype(jnp.int32)
        mine = lax.dynamic_index_in_dim(shards, index, 0, keepdims=False)
        mine_half = lax.dynamic_index_in_dim(halves, index, 0, keepdims=False)
        own = jnp.where(diagonal, jnp.float32(0.0), kernel_block(mine, mine_half, mine, mine_half))
        totals = totals.at[index].add(jnp.sum(own, axis=1))
        row_x = index // N_GY
        row_y = index % N_GY
        for step in range(ROUNDS):
            partner = (((row_x + step % 2) % N_GX) * N_GY + (row_y + step + 1) % N_GY).astype(jnp.int32)
            other = lax.dynamic_index_in_dim(shards, partner, 0, keepdims=False)
            other_half = lax.dynamic_index_in_dim(halves, partner, 0, keepdims=False)
            block = kernel_block(mine, mine_half, other, other_half)
            totals = totals.at[index].add(jnp.sum(block, axis=1))
            totals = totals.at[partner].add(jnp.sum(block, axis=0))
        return totals

    totals = lax.fori_loop(0, count, per_device, jnp.zeros((count, ROWS), jnp.float32))
    return (halves + jnp.log(totals)).reshape(DOCS)
```

```python
import jax
import jax.numpy as jnp
from jax import lax
from jax.sharding import PartitionSpec as P

BAND = 64
AXES = ("gx", "gy")
NX, NY, NZ = 4, 4, 8

DEVICES = [
    (x, y, z, c) for x in range(NX) for y in range(NY) for z in range(NZ) for c in range(2)
]


def number(x, y, z, c):
    x, y, z = x % NX, y % NY, z % NZ
    return (2 * x + z % 2) * 32 + 8 * y + 2 * (z // 2) + c


def is_first(x, y, z, c):
    return c != z % 2


def hop_one(x, y, z, c):
    return (x, y, z + 1, c) if c else (x, y, z - 1, c)


def hop_two(x, y, z, c):
    if c:
        t = (z + 1) % NZ
        return (x, y - (t in (3, 5)) + (t == 0), t, c)
    t = (z - 1) % NZ
    return (x, y + (t in (0, 2, 4)), t, c)


def hop_three(x, y, z, c):
    return (x, y, z - 1, c) if c else (x, y + (z in (6, 7)), z + 1, c)


def own_across(x, y, z, c):
    if not is_first(x, y, z, c):
        return (x, y, z, 1 - c)
    return (x, y + 1, z, 0) if c else (x, y - (z in (1, 3, 5)), z, 1)


def own_along_x(x, y, z, c):
    if not is_first(x, y, z, c):
        return None
    return (x - 1, y - (z == 0), z, c) if c else (x + 1, y + (z == 7), z, c)


def two_along_x(x, y, z, c):
    if is_first(x, y, z, c):
        return None
    return (x + 1, y + 1, z, c) if c else (x - 1, y - 1, z, c)


def two_across(x, y, z, c):
    if not is_first(x, y, z, c):
        return None
    return (x, y + 1, z, 0) if c else (x, y - 1, z, 1)


def three_across(x, y, z, c):
    if is_first(x, y, z, c):
        return None
    return (x, y, z, 1 - c)


def route(*hops):
    pairs = []
    for source in DEVICES:
        at = source
        for hop in hops:
            at = at and hop(*at)
            at = at and (at[0] % NX, at[1] % NY, at[2] % NZ, at[3])
        if at:
            pairs.append((number(*source), number(*at)))
    return pairs


def back(pairs):
    return [(target, source) for source, target in pairs]


def move(value, pairs):
    return lax.ppermute(value, AXES, pairs)


def half_norms(block):
    values = block.astype(jnp.float32)
    return jnp.sum(values * values, axis=1) / (2.0 * BAND)


def kernel_block(left, left_half, right, right_half):
    inner = lax.dot_general(
        left, right, (((1,), (1,)), ((), ())), preferred_element_type=jnp.float32
    )
    return jnp.exp(inner / BAND - left_half[:, None] - right_half[None, :])


def sums(left, left_half, right, right_half):
    block = kernel_block(left, left_half, right, right_half)
    return jnp.sum(block, axis=1), jnp.sum(block, axis=0)


def body(own):
    rows = own.shape[0]
    first = lax.axis_index("gx") % 2 != lax.axis_index("gy") % 2

    def pick(a, b):
        return jnp.where(first, a, b)

    one = move(own, route(hop_one))
    across = move(own, route(own_across))
    along = move(own, route(own_along_x))
    own_late, _ = lax.optimization_barrier((own, one))
    two = move(one, route(hop_two))
    three = move(own_late, route(hop_three))
    two_c = move(two, route(two_across))
    two_x = move(two, route(two_along_x))
    three_c = move(three, route(three_across))

    own_half = half_norms(own)
    diagonal = lax.broadcasted_iota(jnp.int32, (rows, rows), 0) == lax.broadcasted_iota(
        jnp.int32, (rows, rows), 1
    )
    same = jnp.where(diagonal, jnp.float32(0.0), kernel_block(own, own_half, own, own_half))
    total = jnp.sum(same, axis=1)

    two_half = half_norms(two)
    b_left, b_right = sums(
        across, half_norms(across), pick(own, two), pick(own_half, two_half)
    )
    c_block, c_other = pick(along, two_c), pick(one, two)
    c_left, c_right = sums(c_block, half_norms(c_block), c_other, half_norms(c_other))
    three_half = half_norms(three)
    d_left, d_right = sums(three, three_half, two, two_half)
    e_block = pick(three_c, two_x)
    e_left, e_right = sums(e_block, half_norms(e_block), three, three_half)

    zero = jnp.zeros_like(total)
    total = total + pick(b_right, zero)
    total = total + move(b_left, back(route(own_across)))
    total = total + move(c_left, back(route(own_along_x)))
    one_pairs = [p for p in route(hop_one) if is_first(*PLACE[p[1]])]
    total = total + move(
        pick(c_right, c_left), back(one_pairs + route(hop_one, hop_two, two_across))
    )
    total = total + move(
        d_right + pick(zero, b_right + c_right), back(route(hop_one, hop_two))
    )
    total = total + move(d_left + e_right, back(route(hop_three)))
    total = total + move(
        e_left, back(route(hop_three, three_across) + route(hop_one, hop_two, two_along_x))
    )
    return own_half + jnp.log(total)


PLACE = {number(*device): device for device in DEVICES}


def solution(mesh):
    in_specs = (P(AXES, None),)
    return jax.shard_map(
        body, mesh=mesh, in_specs=in_specs, out_specs=P(AXES), check_vma=False
    )
```

```python
import jax
import jax.numpy as jnp
from jax import lax
from jax.sharding import PartitionSpec as P

BAND = 64
AXES = ("gx", "gy")
NX, NY, NZ = 4, 4, 8

DEVICES = [
    (x, y, z, c) for x in range(NX) for y in range(NY) for z in range(NZ) for c in range(2)
]


def number(x, y, z, c):
    x, y, z = x % NX, y % NY, z % NZ
    return (2 * x + z % 2) * 32 + 8 * y + 2 * (z // 2) + c


def is_first(x, y, z, c):
    return c != z % 2


def hop_one(x, y, z, c):
    return (x, y, z + 1, c) if c else (x, y, z - 1, c)


def hop_two(x, y, z, c):
    if c:
        t = (z + 1) % NZ
        return (x, y - (t in (3, 5)), t, c)
    t = (z - 1) % NZ
    return (x, y + (t in (2, 4)), t, c)


def hop_three(x, y, z, c):
    return (x, y - (z == 1), z - 1, c) if c else (x, y + (z == 6), z + 1, c)


def own_across(x, y, z, c):
    if not is_first(x, y, z, c):
        return (x, y, z, 1 - c)
    return (x, y + (z in (2, 4, 6)), z, 0) if c else (x, y - (z in (1, 3, 5)), z, 1)


def own_along_x(x, y, z, c):
    if not is_first(x, y, z, c):
        return None
    return (x - 1, y - (z == 0), z, c) if c else (x + 1, y + (z == 7), z, c)


def two_along_x(x, y, z, c):
    if is_first(x, y, z, c):
        return None
    return (x + 1, y + 1, z, c) if c else (x - 1, y - 1, z, c)


def two_across(x, y, z, c):
    if not is_first(x, y, z, c):
        return None
    return (x, y + 1, z, 0) if c else (x, y - 1, z, 1)


def three_across(x, y, z, c):
    if is_first(x, y, z, c):
        return None
    return (x, y, z, 1 - c)


def route(*hops):
    pairs = []
    for source in DEVICES:
        at = source
        for hop in hops:
            at = at and hop(*at)
            at = at and (at[0] % NX, at[1] % NY, at[2] % NZ, at[3])
        if at:
            pairs.append((number(*source), number(*at)))
    return pairs


def back(pairs):
    return [(target, source) for source, target in pairs]


def move(value, pairs):
    return lax.ppermute(value, AXES, pairs)


def half_norms(block):
    values = block.astype(jnp.float32)
    return jnp.sum(values * values, axis=1) / (2.0 * BAND)


def kernel_block(left, left_half, right, right_half):
    inner = lax.dot_general(
        left, right, (((1,), (1,)), ((), ())), preferred_element_type=jnp.float32
    )
    return jnp.exp(inner / BAND - left_half[:, None] - right_half[None, :])


def sums(left, left_half, right, right_half):
    block = kernel_block(left, left_half, right, right_half)
    return jnp.sum(block, axis=1), jnp.sum(block, axis=0)


def after(value, *others):
    return lax.optimization_barrier((value, *others))[0]


def body(own):
    rows = own.shape[0]
    half = rows // 2
    first = lax.axis_index("gx") % 2 != lax.axis_index("gy") % 2

    def pick(a, b):
        return jnp.where(first, a, b)

    own_a, own_b = own[:half], own[half:]
    one_a = move(own_a, route(hop_one))
    one_b = move(own_b, route(hop_one))
    across = move(own, route(own_across))
    along = move(own, route(own_along_x))

    own_half = half_norms(own)
    diagonal = lax.broadcasted_iota(jnp.int32, (rows, rows), 0) == lax.broadcasted_iota(
        jnp.int32, (rows, rows), 1
    )
    same = jnp.where(diagonal, jnp.float32(0.0), kernel_block(own, own_half, own, own_half))
    total = jnp.sum(same, axis=1)
    two_a = move(one_a, route(hop_two))
    two_b = move(after(one_b, across, along, total), route(hop_two))

    three_a = move(after(own_a, two_a), route(hop_three))
    two_c_a = move(two_a, route(two_across))
    two_x_a = move(two_a, route(two_along_x))
    three_b = move(after(own_b, two_b), route(hop_three))
    two_c_b = move(after(two_b, two_c_a), route(two_across))
    two_x_b = move(after(two_b, two_x_a), route(two_along_x))

    one = jnp.concatenate([one_a, one_b])
    two = jnp.concatenate([two_a, two_b])
    two_half = half_norms(two)
    b_left, b_right = sums(
        across, half_norms(across), pick(own, two), pick(own_half, two_half)
    )
    c_block = pick(along, jnp.concatenate([two_c_a, two_c_b]))
    c_other = pick(one, two)
    c_left, c_right = sums(c_block, half_norms(c_block), c_other, half_norms(c_other))
    three_a_half = half_norms(three_a)
    three_c_a = move(three_a, route(three_across))
    d_left_a, d_right_a = sums(three_a, three_a_half, two, two_half)
    e_a = pick(three_c_a, two_x_a)
    e_a_half = half_norms(e_a)
    e_left_a, e_right_a = sums(e_a, e_a_half, three_a, three_a_half)

    three_b, two, e_a, _ = lax.optimization_barrier(
        (three_b, two, e_a, (b_left, c_left, d_left_a, e_left_a))
    )
    three_c_b = move(three_b, route(three_across))
    three_b_half = half_norms(three_b)
    d_left_b, d_right_b = sums(three_b, three_b_half, two, two_half)
    e_left_c, e_right_b = sums(e_a, e_a_half, three_b, three_b_half)
    three = jnp.concatenate([three_a, three_b])
    three_half = jnp.concatenate([three_a_half, three_b_half])
    e_b = pick(three_c_b, two_x_b)
    e_left_b, e_right = sums(e_b, half_norms(e_b), three, three_half)

    zero = jnp.zeros_like(total)
    total = total + pick(b_right, zero)
    b_left, c_left, _ = lax.optimization_barrier((b_left, c_left, (two_c_b, two_x_b)))
    total = total + move(b_left, back(route(own_across)))
    total = total + move(c_left, back(route(own_along_x)))
    one_pairs = [p for p in route(hop_one) if is_first(*PLACE[p[1]])]
    total = total + move(
        pick(c_right, c_left), back(one_pairs + route(hop_one, hop_two, two_across))
    )
    total = total + move(
        d_right_a + d_right_b + pick(zero, b_right + c_right), back(route(hop_one, hop_two))
    )
    total = total + move(
        jnp.concatenate([d_left_a + e_right_a, d_left_b + e_right_b]) + e_right,
        back(route(hop_three)),
    )
    total = total + move(
        jnp.concatenate([e_left_a + e_left_c, e_left_b]),
        back(route(hop_three, three_across) + route(hop_one, hop_two, two_along_x)),
    )
    return own_half + jnp.log(total)


PLACE = {number(*device): device for device in DEVICES}


def solution(mesh):
    in_specs = (P(AXES, None),)
    return jax.shard_map(
        body, mesh=mesh, in_specs=in_specs, out_specs=P(AXES), check_vma=False
    )
```

```python
import functools
import math

import jax
import jax.numpy as jnp
from jax import lax
from jax.experimental import pallas as pl
from jax.experimental.pallas import tpu as pltpu
from jax.sharding import PartitionSpec as P

BAND = 64
LOG2E = math.log2(math.e)
HALF = 512
TILE = 256
LANES = 128
AXES = ("gx", "gy")
NX, NY, NZ = 4, 4, 8

DEVICES = [
    (x, y, z, c) for x in range(NX) for y in range(NY) for z in range(NZ) for c in range(2)
]


def number(x, y, z, c):
    x, y, z = x % NX, y % NY, z % NZ
    return (2 * x + z % 2) * 32 + 8 * y + 2 * (z // 2) + c


def is_first(x, y, z, c):
    return c != z % 2


def hop_one(x, y, z, c):
    return (x, y, z + 1, c) if c else (x, y, z - 1, c)


def hop_two(x, y, z, c):
    if c:
        t = (z + 1) % NZ
        return (x, y - (t in (3, 5)), t, c)
    t = (z - 1) % NZ
    return (x, y + (t in (2, 4)), t, c)


def hop_three(x, y, z, c):
    return (x, y, z - 1, c) if c else (x, y, z + 1, c)


def is_seam(x, y, z, c):
    return (z, c) in ((1, 1), (6, 0))


def own_across(x, y, z, c):
    if not is_first(x, y, z, c):
        return (x, y, z, 1 - c)
    return (x, y + (z in (2, 4, 6)), z, 0) if c else (x, y - (z in (1, 3, 5)), z, 1)


def own_in_plane(x, y, z, c):
    if is_first(x, y, z, c):
        return (x - 1, y - (z == 0), z, c) if c else (x + 1, y + (z == 7), z, c)
    if is_seam(x, y, z, c):
        return (x, y - 1, z, c) if c else (x, y + 1, z, c)
    return None


def two_along_x(x, y, z, c):
    if is_first(x, y, z, c):
        return None
    return (x + 1, y + 1, z, c) if c else (x - 1, y - 1, z, c)


def two_across(x, y, z, c):
    if not is_first(x, y, z, c):
        return None
    return (x, y + 1, z, 0) if c else (x, y - 1, z, 1)


def three_across(x, y, z, c):
    if is_first(x, y, z, c):
        return None
    return (x, y, z, 1 - c)


def route(*hops):
    pairs = []
    for source in DEVICES:
        at = source
        for hop in hops:
            at = at and hop(*at)
            at = at and (at[0] % NX, at[1] % NY, at[2] % NZ, at[3])
        if at:
            pairs.append((number(*source), number(*at)))
    return pairs


def back(pairs):
    return [(target, source) for source, target in pairs]


def move(value, pairs):
    return lax.ppermute(value, AXES, pairs)


def half_norms(block):
    values = block.astype(jnp.float32)
    return jnp.sum(values * values, axis=1) / (2.0 * BAND)


def kernel_block(left, left_half, right, right_half):
    inner = lax.dot_general(
        left, right, (((1,), (1,)), ((), ())), preferred_element_type=jnp.float32
    )
    return jnp.exp(inner / BAND - left_half[:, None] - right_half[None, :])


def lane_sums(values):
    return functools.reduce(
        lambda x, y: x + y,
        [values[:, i : i + LANES] for i in range(0, values.shape[1], LANES)],
    )


def as_row(partial):
    return jnp.sum(jnp.transpose(partial), axis=0, keepdims=True)


def pairs_kernel(jobs_first, jobs_second, names, places, outs, flag, *refs):
    count = len(names)
    sources = dict(zip(names, refs[:count]))
    results = dict(zip(outs, refs[count : count + len(outs)]))
    blocks, norms, totals, sems = refs[count + len(outs) :]

    def run(jobs):
        order = []
        for job in jobs:
            order += [part for part in job if part not in order]
        slot = {part: i for i, part in enumerate(order)}
        copies = {}
        for part in order:
            name, offset = places[part]
            copies[part] = pltpu.make_async_copy(
                sources[name].at[pl.ds(offset, HALF)], blocks.at[slot[part]], sems.at[slot[part]]
            )
            copies[part].start()
        lefts = [part for part in order if any(part == job[0] for job in jobs)]
        rights, ready, seen = {}, set(), set()
        for left, right in jobs:
            for part in (left, right):
                if part not in ready:
                    copies[part].wait()
                    ready.add(part)
                    values = blocks[slot[part]].astype(jnp.float32)
                    squares = lane_sums(values * values) * (LOG2E / (2.0 * BAND))
                    if part in lefts:
                        norms[slot[part]] = jnp.broadcast_to(
                            jnp.sum(squares, axis=1, keepdims=True), (HALF, LANES)
                        )
                    if any(part == job[1] for job in jobs):
                        rights[part] = as_row(squares)
            for at in range(0, HALF, TILE):
                inner = lax.dot_general(
                    blocks[slot[left]],
                    blocks[slot[right], at : at + TILE],
                    (((1,), (1,)), ((), ())),
                    preferred_element_type=jnp.float32,
                )
                rows = None
                for lane in range(0, TILE, LANES):
                    cut = slice(at + lane, at + lane + LANES)
                    value = jnp.exp2(
                        inner[:, lane : lane + LANES] * (LOG2E / BAND)
                        - norms[slot[left]]
                        - rights[right][:, cut]
                    )
                    rows = value if rows is None else rows + value
                    column = jnp.sum(value, axis=0, keepdims=True)
                    if (right, cut.start) in seen:
                        results[right][:, cut] += column
                    else:
                        seen.add((right, cut.start))
                        results[right][:, cut] = column
                if left in seen:
                    totals[slot[left]] += rows
                else:
                    seen.add(left)
                    totals[slot[left]] = rows
        for part in lefts:
            results[part][...] = as_row(totals[slot[part]])
        for part in outs:
            if part not in order:
                results[part][...] = jnp.zeros_like(results[part])

    @pl.when(flag[0] == 1)
    def _():
        run(jobs_first)

    @pl.when(flag[0] != 1)
    def _():
        run(jobs_second)


def pair_sums(flag, arrays, jobs_first, jobs_second):
    names = list(arrays)
    places = {}
    for name in names:
        if arrays[name].shape[0] == HALF:
            places[name] = (name, 0)
        else:
            places[name + "0"], places[name + "1"] = (name, 0), (name, HALF)
    used = [sorted({p for job in jobs for p in job}) for jobs in (jobs_first, jobs_second)]
    outs = sorted(set(used[0]) | set(used[1]))
    slots = max(len(u) for u in used)
    results = pl.pallas_call(
        functools.partial(pairs_kernel, jobs_first, jobs_second, names, places, outs),
        out_shape=[jax.ShapeDtypeStruct((1, HALF), jnp.float32) for _ in outs],
        in_specs=[pl.BlockSpec(memory_space=pltpu.SMEM)]
        + [pl.BlockSpec(memory_space=pltpu.HBM)] * len(names),
        out_specs=[pl.BlockSpec(memory_space=pltpu.VMEM)] * len(outs),
        scratch_shapes=[
            pltpu.VMEM((slots, HALF, 1024), jnp.bfloat16),
            pltpu.VMEM((slots, HALF, LANES), jnp.float32),
            pltpu.VMEM((slots, HALF, LANES), jnp.float32),
            pltpu.SemaphoreType.DMA((slots,)),
        ],
        compiler_params=pltpu.CompilerParams(vmem_limit_bytes=32 * 1024 * 1024),
        cost_estimate=pl.CostEstimate(flops=1, bytes_accessed=1, transcendentals=0),
    )(flag, *[arrays[name] for name in names])
    return dict(zip(outs, results))


def both(lefts, rights):
    return [(left, right) for left in lefts for right in rights]


def whole(first_half, second_half):
    return jnp.concatenate([first_half[0], second_half[0]])


def after(value, *others):
    return lax.optimization_barrier((value, *others))[0]


def body(own):
    rows = own.shape[0]
    half = rows // 2
    first = lax.axis_index("gx") % 2 != lax.axis_index("gy") % 2

    gx, gy = lax.axis_index("gx"), lax.axis_index("gy")
    height, core = 2 * ((gy % 8) // 2) + gx % 2, gy % 2
    seam = ((height == 1) & (core == 1)) | ((height == 6) & (core == 0))
    flag = first.astype(jnp.int32).reshape(1)
    own_a = own[:half]
    own_b = lax.optimization_barrier(after(own, own_a)[half:])
    later = after(own, own_b)
    one_a = move(own_a, route(hop_one))
    one_b = move(own_b, route(hop_one))
    along = move(later, route(own_in_plane))
    across = move(later, route(own_across))
    two_a = move(one_a, route(hop_two))

    own_half = half_norms(own)
    diagonal = lax.broadcasted_iota(jnp.int32, (rows, rows), 0) == lax.broadcasted_iota(
        jnp.int32, (rows, rows), 1
    )
    same = jnp.where(diagonal, jnp.float32(0.0), kernel_block(own, own_half, own, own_half))
    total = jnp.sum(same, axis=1)
    two_b = move(after(one_b, total, own_half), route(hop_two))
    third_a, third_b = lax.optimization_barrier(
        (
            jnp.where(seam, along[:half], own[:half]),
            jnp.where(seam, along[half:], own[half:]),
        )
    )
    early = pair_sums(
        flag,
        dict(along=along, one_a=one_a, one_b=one_b),
        both(["along0", "along1"], ["one_a", "one_b"]),
        [],
    )

    two_a_after = after(two_a, early)
    two_c_a = move(two_a_after, route(two_across))
    two_x_a = move(two_a_after, route(two_along_x))
    three_a = move(after(third_a, two_a), route(hop_three))
    three_b = move(after(third_b, two_b), route(hop_three))
    two_c_b = move(two_b, route(two_across))
    two_x_b = move(after(two_b, two_x_a), route(two_along_x))

    middle = pair_sums(
        flag,
        dict(own=own, across=after(across, three_a), two_a=two_a, two_b=two_b, two_c_a=two_c_a),
        both(["own0", "own1"], ["across0", "across1"]),
        both(["across0", "across1", "two_c_a"], ["two_a", "two_b"]),
    )
    three_c_a = move(three_a, route(three_across))
    late = pair_sums(
        flag,
        dict(
            three_a=three_a, two_a=two_a, two_b=two_b, two_c_b=two_c_b, two_x_a=two_x_a,
            three_c_a=three_c_a,
        ),
        both(["three_a"], ["two_a", "two_b", "three_c_a"]),
        both(["three_a"], ["two_a", "two_b", "two_x_a"]) + both(["two_c_b"], ["two_a", "two_b"]),
    )

    held = dict(route(own_in_plane))
    ahead = dict(route(hop_three))
    third = [(s, ahead[held[s] if is_seam(*PLACE[s]) else s]) for s in PLACE]
    over = dict(route(three_across))
    crossed = [(s, over[t]) for s, t in third if t in over]
    along_pairs = [p for p in route(own_in_plane) if is_first(*PLACE[p[1]])]
    one_pairs = [p for p in route(hop_one) if is_first(*PLACE[p[1]])]
    along_sums = move(whole(early["along0"], early["along1"]), back(along_pairs))
    across_sums = move(
        whole(middle["across0"], middle["across1"]), back(route(own_across))
    )

    three_b, _ = lax.optimization_barrier((three_b, (late, along_sums, across_sums)))
    three_c_b = move(three_b, route(three_across))
    last = pair_sums(
        flag,
        dict(
            three_b=three_b, two_a=two_a, two_b=two_b, two_x_a=two_x_a, two_x_b=two_x_b,
            three_a=three_a, three_c_a=three_c_a,
        ),
        both(["three_b"], ["two_a", "two_b", "three_c_a"]),
        both(["three_b"], ["two_a", "two_b", "two_x_a"]) + both(["three_a", "three_b"], ["two_x_b"]),
    )
    final = pair_sums(
        flag,
        dict(three_a=three_a, three_b=three_b, three_c_b=three_c_b),
        both(["three_a", "three_b"], ["three_c_b"]),
        [],
    )

    total = total + whole(middle["own0"], middle["own1"])
    total = total + along_sums + across_sums
    total = total + move(
        after(
            whole(early["one_a"] + middle["two_c_a"], early["one_b"] + late["two_c_b"]), last
        ),
        back(one_pairs + route(hop_one, hop_two, two_across)),
    )
    total = total + move(
        whole(
            middle["two_a"] + late["two_a"] + last["two_a"],
            middle["two_b"] + late["two_b"] + last["two_b"],
        ),
        back(route(hop_one, hop_two)),
    )
    total = total + move(
        whole(
            late["three_a"] + last["three_a"] + final["three_a"],
            last["three_b"] + final["three_b"],
        ),
        back(third),
    )
    total = total + move(
        whole(
            late["two_x_a"] + last["two_x_a"] + late["three_c_a"] + last["three_c_a"],
            last["two_x_b"] + final["three_c_b"],
        ),
        back(crossed + route(hop_one, hop_two, two_along_x)),
    )
    return own_half + jnp.log(total)


PLACE = {number(*device): device for device in DEVICES}


def solution(mesh):
    in_specs = (P(AXES, None),)
    return jax.shard_map(
        body, mesh=mesh, in_specs=in_specs, out_specs=P(AXES), check_vma=False
    )
```

```python
import functools
import math

import jax
import jax.numpy as jnp
from jax import lax
from jax.experimental import pallas as pl
from jax.experimental.pallas import tpu as pltpu
from jax.sharding import PartitionSpec as P

BAND = 64
LOG2E = math.log2(math.e)
HALF = 512
TILE = 256
LANES = 128
AXES = ("gx", "gy")
NX, NY, NZ = 4, 4, 8

DEVICES = [
    (x, y, z, c) for x in range(NX) for y in range(NY) for z in range(NZ) for c in range(2)
]


def number(x, y, z, c):
    x, y, z = x % NX, y % NY, z % NZ
    return (2 * x + z % 2) * 32 + 8 * y + 2 * (z // 2) + c


def is_first(x, y, z, c):
    return c != z % 2


def hop_one(x, y, z, c):
    return (x, y, z + 1, c) if c else (x, y, z - 1, c)


def hop_two(x, y, z, c):
    if c:
        t = (z + 1) % NZ
        return (x, y - (t in (3, 5)), t, c)
    t = (z - 1) % NZ
    return (x, y + (t in (2, 4)), t, c)


def hop_three(x, y, z, c):
    return (x, y, z - 1, c) if c else (x, y, z + 1, c)


def is_seam(x, y, z, c):
    return (z, c) in ((1, 1), (6, 0))


def own_across(x, y, z, c):
    if not is_first(x, y, z, c):
        return (x, y, z, 1 - c)
    return (x, y + (z in (2, 4, 6)), z, 0) if c else (x, y - (z in (1, 3, 5)), z, 1)


def own_in_plane(x, y, z, c):
    if is_first(x, y, z, c):
        return (x - 1, y - (z == 0), z, c) if c else (x + 1, y + (z == 7), z, c)
    if is_seam(x, y, z, c):
        return (x, y - 1, z, c) if c else (x, y + 1, z, c)
    return None


def two_along_x(x, y, z, c):
    if is_first(x, y, z, c):
        return None
    return (x + 1, y + 1, z, c) if c else (x - 1, y - 1, z, c)


def two_across(x, y, z, c):
    if not is_first(x, y, z, c):
        return None
    return (x, y + 1, z, 0) if c else (x, y - 1, z, 1)


def three_across(x, y, z, c):
    if is_first(x, y, z, c):
        return None
    return (x, y, z, 1 - c)


def route(*hops):
    pairs = []
    for source in DEVICES:
        at = source
        for hop in hops:
            at = at and hop(*at)
            at = at and (at[0] % NX, at[1] % NY, at[2] % NZ, at[3])
        if at:
            pairs.append((number(*source), number(*at)))
    return pairs


def back(pairs):
    return [(target, source) for source, target in pairs]


def move(value, pairs):
    return lax.ppermute(value, AXES, pairs)


def half_norms(block):
    values = block.astype(jnp.float32)
    return jnp.sum(values * values, axis=1) / (2.0 * BAND)


def kernel_block(left, left_half, right, right_half):
    inner = lax.dot_general(
        left, right, (((1,), (1,)), ((), ())), preferred_element_type=jnp.float32
    )
    return jnp.exp(inner / BAND - left_half[:, None] - right_half[None, :])


def lane_sums(values):
    return functools.reduce(
        lambda x, y: x + y,
        [values[:, i : i + LANES] for i in range(0, values.shape[1], LANES)],
    )


def as_row(partial):
    return jnp.sum(jnp.transpose(partial), axis=0, keepdims=True)


def pairs_kernel(parts_of, lefts_of, names, places, outs, has_single, flag, jobs, *refs):
    sources = dict(zip(names, refs[: len(names)]))
    results = dict(zip(outs, refs[len(names) : len(names) + len(outs)]))
    blocks, norms, rights, totals, sums, sems = refs[len(names) + len(outs) :]
    variant = flag[0]
    lefts = jnp.where(variant == 1, lefts_of[1], lefts_of[0])
    halves = jnp.where(variant == 1, len(parts_of[1]), len(parts_of[0]))

    for which in (0, 1):

        @pl.when(variant == which)
        def _(which=which):
            for slot, part in enumerate(parts_of[which]):
                name, offset = places[part]
                pltpu.make_async_copy(
                    sources[name].at[pl.ds(offset, HALF)], blocks.at[slot], sems.at[slot]
                ).start()

    def squares(slot):
        pltpu.make_async_copy(blocks.at[slot], blocks.at[slot], sems.at[slot]).wait()
        values = blocks[slot].astype(jnp.float32)
        return lane_sums(values * values) * (LOG2E / (2.0 * BAND))

    def prepare_left(slot, carry):
        norms[slot] = jnp.broadcast_to(
            jnp.sum(squares(slot), axis=1, keepdims=True), (HALF, LANES)
        )
        totals[slot] = jnp.zeros((HALF, LANES), jnp.float32)
        return carry

    def prepare_right(slot, carry):
        rights[slot] = as_row(squares(slot))
        sums[slot] = jnp.zeros((1, HALF), jnp.float32)
        return carry

    lax.fori_loop(0, lefts, prepare_left, 0)
    lax.fori_loop(lefts, halves, prepare_right, 0)

    def pair(left, right_slots):
        for right in right_slots:
            for at in range(0, HALF, TILE):
                inner = lax.dot_general(
                    blocks[left],
                    blocks[right, at : at + TILE],
                    (((1,), (1,)), ((), ())),
                    preferred_element_type=jnp.float32,
                )
                rows = None
                for lane in range(0, TILE, LANES):
                    cut = slice(at + lane, at + lane + LANES)
                    value = jnp.exp2(
                        inner[:, lane : lane + LANES] * (LOG2E / BAND)
                        - norms[left]
                        - rights[right, :, cut]
                    )
                    rows = value if rows is None else rows + value
                    sums[right, :, cut] += jnp.sum(value, axis=0, keepdims=True)
                totals[left] += rows

    def double(job, carry):
        pair(jobs[variant, 3 * job], (jobs[variant, 3 * job + 1], jobs[variant, 3 * job + 2]))
        return carry

    lax.fori_loop(0, jobs[variant, jobs.shape[1] - 1], double, 0)
    if has_single:
        single = jobs.shape[1] - 3

        @pl.when(jobs[variant, single] >= 0)
        def _():
            pair(jobs[variant, single], (jobs[variant, single + 1],))

    def finish(slot, carry):
        sums[slot] = as_row(totals[slot])
        return carry

    lax.fori_loop(0, lefts, finish, 0)

    for which in (0, 1):

        @pl.when(variant == which)
        def _(which=which):
            for part in outs:
                if part in parts_of[which]:
                    results[part][...] = sums[parts_of[which].index(part)]
                else:
                    results[part][...] = jnp.zeros_like(results[part])


def pair_sums(flag, arrays, jobs_first, jobs_second):
    names = list(arrays)
    places = {}
    for name in names:
        if arrays[name].shape[0] == HALF:
            places[name] = (name, 0)
        else:
            places[name + "0"], places[name + "1"] = (name, 0), (name, HALF)
    parts_of, lefts_of, rows = [], [], []
    lists = (jobs_second, jobs_first)
    most = max(len(jobs) for jobs in lists)
    for jobs in lists:
        left_parts = list(dict.fromkeys(job[0] for job in jobs))
        right_parts = list(dict.fromkeys(part for job in jobs for part in job[1:]))
        order = left_parts + right_parts
        parts_of.append(order)
        lefts_of.append(len(left_parts))
        doubles = [job for job in jobs if len(job) == 3]
        singles = [job for job in jobs if len(job) == 2]
        row = [order.index(part) for job in doubles for part in job]
        row += [0] * (3 * most - len(row))
        row += [order.index(part) for part in singles[0]] if singles else [-1, 0]
        rows.append(row + [len(doubles)])
    outs = sorted(set(parts_of[0]) | set(parts_of[1]))
    slots = max(len(order) for order in parts_of)
    has_single = any(len(job) == 2 for jobs in lists for job in jobs)
    smem = pl.BlockSpec(memory_space=pltpu.SMEM)
    results = pl.pallas_call(
        functools.partial(
            pairs_kernel, parts_of, lefts_of, names, places, outs, has_single
        ),
        out_shape=[jax.ShapeDtypeStruct((1, HALF), jnp.float32) for _ in outs],
        in_specs=[smem, smem] + [pl.BlockSpec(memory_space=pltpu.HBM)] * len(names),
        out_specs=[pl.BlockSpec(memory_space=pltpu.VMEM)] * len(outs),
        scratch_shapes=[
            pltpu.VMEM((slots, HALF, 1024), jnp.bfloat16),
            pltpu.VMEM((slots, HALF, LANES), jnp.float32),
            pltpu.VMEM((slots, 1, HALF), jnp.float32),
            pltpu.VMEM((slots, HALF, LANES), jnp.float32),
            pltpu.VMEM((slots, 1, HALF), jnp.float32),
            pltpu.SemaphoreType.DMA((slots,)),
        ],
        compiler_params=pltpu.CompilerParams(vmem_limit_bytes=32 * 1024 * 1024),
        cost_estimate=pl.CostEstimate(flops=1, bytes_accessed=1, transcendentals=0),
    )(flag, jnp.asarray(rows, jnp.int32), *[arrays[name] for name in names])
    return dict(zip(outs, results))


def both(lefts, first_right, second_right):
    return [(left, first_right, second_right) for left in lefts]


def whole(first_half, second_half):
    return jnp.concatenate([first_half[0], second_half[0]])


def after(value, *others):
    return lax.optimization_barrier((value, *others))[0]


def body(own):
    rows = own.shape[0]
    half = rows // 2
    first = lax.axis_index("gx") % 2 != lax.axis_index("gy") % 2

    gx, gy = lax.axis_index("gx"), lax.axis_index("gy")
    height, core = 2 * ((gy % 8) // 2) + gx % 2, gy % 2
    seam = ((height == 1) & (core == 1)) | ((height == 6) & (core == 0))
    flag = first.astype(jnp.int32).reshape(1)
    own_a = own[:half]
    own_b = lax.optimization_barrier(after(own, own_a)[half:])
    later = after(own, own_b)
    one_a = move(own_a, route(hop_one))
    one_b = move(own_b, route(hop_one))
    along = move(later, route(own_in_plane))
    across = move(later, route(own_across))
    two_a = move(one_a, route(hop_two))

    own_half = half_norms(own)
    diagonal = lax.broadcasted_iota(jnp.int32, (rows, rows), 0) == lax.broadcasted_iota(
        jnp.int32, (rows, rows), 1
    )
    same = jnp.where(diagonal, jnp.float32(0.0), kernel_block(own, own_half, own, own_half))
    total = jnp.sum(same, axis=1)
    two_b = move(after(one_b, total, own_half), route(hop_two))
    third_a, third_b = lax.optimization_barrier(
        (
            jnp.where(seam, along[:half], own[:half]),
            jnp.where(seam, along[half:], own[half:]),
        )
    )
    early = pair_sums(
        flag,
        dict(along=along, one_a=one_a, one_b=one_b),
        both(["along0", "along1"], "one_a", "one_b"),
        [],
    )

    two_a_after = after(two_a, early)
    two_c_a = move(two_a_after, route(two_across))
    two_x_a = move(two_a_after, route(two_along_x))
    three_a = move(after(third_a, two_a), route(hop_three))
    three_b = move(after(third_b, two_b), route(hop_three))
    two_c_b = move(two_b, route(two_across))
    two_x_b = move(after(two_b, two_x_a), route(two_along_x))

    middle = pair_sums(
        flag,
        dict(own=own, across=after(across, three_a), two_a=two_a, two_b=two_b, two_c_a=two_c_a),
        both(["own0", "own1"], "across0", "across1"),
        both(["across0", "across1", "two_c_a"], "two_a", "two_b"),
    )
    three_c_a = move(three_a, route(three_across))
    late = pair_sums(
        flag,
        dict(
            three_a=three_a, two_a=two_a, two_b=two_b, two_c_b=two_c_b, two_x_a=two_x_a,
            three_c_a=three_c_a,
        ),
        both(["three_a"], "two_a", "two_b") + [("three_a", "three_c_a")],
        both(["three_a", "two_c_b"], "two_a", "two_b") + [("three_a", "two_x_a")],
    )

    held = dict(route(own_in_plane))
    ahead = dict(route(hop_three))
    third = [(s, ahead[held[s] if is_seam(*PLACE[s]) else s]) for s in PLACE]
    over = dict(route(three_across))
    crossed = [(s, over[t]) for s, t in third if t in over]
    along_pairs = [p for p in route(own_in_plane) if is_first(*PLACE[p[1]])]
    one_pairs = [p for p in route(hop_one) if is_first(*PLACE[p[1]])]
    along_sums = move(whole(early["along0"], early["along1"]), back(along_pairs))
    across_sums = move(
        whole(middle["across0"], middle["across1"]), back(route(own_across))
    )

    three_b, _ = lax.optimization_barrier((three_b, (late, along_sums, across_sums)))
    three_c_b = move(three_b, route(three_across))
    last = pair_sums(
        flag,
        dict(
            three_b=three_b, two_a=two_a, two_b=two_b, two_x_a=two_x_a, two_x_b=two_x_b,
            three_a=three_a, three_c_a=three_c_a,
        ),
        both(["three_b"], "two_a", "two_b") + [("three_b", "three_c_a")],
        both(["three_b"], "two_a", "two_b")
        + both(["three_b"], "two_x_a", "two_x_b")
        + [("three_a", "two_x_b")],
    )
    final = pair_sums(
        flag,
        dict(three_a=three_a, three_b=three_b, three_c_b=three_c_b),
        both(["three_c_b"], "three_a", "three_b"),
        [],
    )

    total = total + whole(middle["own0"], middle["own1"])
    total = total + along_sums + across_sums
    total = total + move(
        after(
            whole(early["one_a"] + middle["two_c_a"], early["one_b"] + late["two_c_b"]), last
        ),
        back(one_pairs + route(hop_one, hop_two, two_across)),
    )
    total = total + move(
        whole(
            middle["two_a"] + late["two_a"] + last["two_a"],
            middle["two_b"] + late["two_b"] + last["two_b"],
        ),
        back(route(hop_one, hop_two)),
    )
    total = total + move(
        whole(
            late["three_a"] + last["three_a"] + final["three_a"],
            last["three_b"] + final["three_b"],
        ),
        back(third),
    )
    total = total + move(
        whole(
            late["two_x_a"] + last["two_x_a"] + late["three_c_a"] + last["three_c_a"],
            last["two_x_b"] + final["three_c_b"],
        ),
        back(crossed + route(hop_one, hop_two, two_along_x)),
    )
    return own_half + jnp.log(total)


PLACE = {number(*device): device for device in DEVICES}


def solution(mesh):
    in_specs = (P(AXES, None),)
    return jax.shard_map(
        body, mesh=mesh, in_specs=in_specs, out_specs=P(AXES), check_vma=False
    )
```

```python
import functools
import math

import jax
import jax.numpy as jnp
from jax import lax
from jax.experimental import pallas as pl
from jax.experimental.pallas import tpu as pltpu
from jax.sharding import PartitionSpec as P

BAND = 64
LOG2E = math.log2(math.e)
HALF = 512
TILE = 256
LANES = 128
AXES = ("gx", "gy")
NX, NY, NZ = 4, 4, 8

DEVICES = [
    (x, y, z, c) for x in range(NX) for y in range(NY) for z in range(NZ) for c in range(2)
]


def number(x, y, z, c):
    x, y, z = x % NX, y % NY, z % NZ
    return (2 * x + z % 2) * 32 + 8 * y + 2 * (z // 2) + c


def is_first(x, y, z, c):
    return c != z % 2


def hop_one(x, y, z, c):
    return (x, y, z + 1, c) if c else (x, y, z - 1, c)


def hop_two(x, y, z, c):
    if c:
        t = (z + 1) % NZ
        return (x, y - (t in (3, 5)), t, c)
    t = (z - 1) % NZ
    return (x, y + (t in (2, 4)), t, c)


def hop_three(x, y, z, c):
    return (x, y, z - 1, c) if c else (x, y, z + 1, c)


def is_seam(x, y, z, c):
    return (z, c) in ((1, 1), (6, 0))


def own_across(x, y, z, c):
    if not is_first(x, y, z, c):
        return (x, y, z, 1 - c)
    return (x, y + (z in (2, 4, 6)), z, 0) if c else (x, y - (z in (1, 3, 5)), z, 1)


def own_in_plane(x, y, z, c):
    if is_first(x, y, z, c):
        return (x - 1, y - (z == 0), z, c) if c else (x + 1, y + (z == 7), z, c)
    if is_seam(x, y, z, c):
        return (x, y - 1, z, c) if c else (x, y + 1, z, c)
    return None


def two_along_x(x, y, z, c):
    if is_first(x, y, z, c):
        return None
    return (x + 1, y + 1, z, c) if c else (x - 1, y - 1, z, c)


def two_across(x, y, z, c):
    if not is_first(x, y, z, c):
        return None
    return (x, y + 1, z, 0) if c else (x, y - 1, z, 1)


def three_across(x, y, z, c):
    if is_first(x, y, z, c):
        return None
    return (x, y, z, 1 - c)


def route(*hops):
    pairs = []
    for source in DEVICES:
        at = source
        for hop in hops:
            at = at and hop(*at)
            at = at and (at[0] % NX, at[1] % NY, at[2] % NZ, at[3])
        if at:
            pairs.append((number(*source), number(*at)))
    return pairs


def back(pairs):
    return [(target, source) for source, target in pairs]


def move(value, pairs):
    return lax.ppermute(value, AXES, pairs)


def half_norms(block):
    values = block.astype(jnp.float32)
    return jnp.sum(values * values, axis=1) / (2.0 * BAND)


def kernel_block(left, left_half, right, right_half):
    inner = lax.dot_general(
        left, right, (((1,), (1,)), ((), ())), preferred_element_type=jnp.float32
    )
    return jnp.exp(inner / BAND - left_half[:, None] - right_half[None, :])


def lane_sums(values):
    return functools.reduce(
        lambda x, y: x + y,
        [values[:, i : i + LANES] for i in range(0, values.shape[1], LANES)],
    )


def as_row(partial):
    return jnp.sum(jnp.transpose(partial), axis=0, keepdims=True)


def pairs_kernel(parts_of, jobs, names, places, outs, flag, *refs):
    sources = dict(zip(names, refs[: len(names)]))
    results = dict(zip(outs, refs[len(names) : len(names) + len(outs)]))
    blocks, norms, rights, totals, sums, sems = refs[len(names) + len(outs) :]
    variant = flag[0]
    lefts = {job[1] for job in jobs}

    for which in (0, 1):

        @pl.when(variant == which)
        def _(which=which):
            for slot, part in parts_of[which].items():
                name, offset = places[part]
                pltpu.make_async_copy(
                    sources[name].at[pl.ds(offset, HALF)], blocks.at[slot], sems.at[slot]
                ).start()

    def prepare(slot):
        pltpu.make_async_copy(blocks.at[slot], blocks.at[slot], sems.at[slot]).wait()
        values = blocks[slot].astype(jnp.float32)
        squares = lane_sums(values * values) * (LOG2E / (2.0 * BAND))
        if slot in lefts:
            norms[slot] = jnp.broadcast_to(
                jnp.sum(squares, axis=1, keepdims=True), (HALF, LANES)
            )
        else:
            rights[slot] = as_row(squares)

    def pair(left, right, seen):
        for at in range(0, HALF, TILE):
            inner = lax.dot_general(
                blocks[left],
                blocks[right, at : at + TILE],
                (((1,), (1,)), ((), ())),
                preferred_element_type=jnp.float32,
            )
            rows = None
            for lane in range(0, TILE, LANES):
                cut = slice(at + lane, at + lane + LANES)
                value = jnp.exp2(
                    inner[:, lane : lane + LANES] * (LOG2E / BAND)
                    - norms[left]
                    - rights[right, :, cut]
                )
                rows = value if rows is None else rows + value
                column = jnp.sum(value, axis=0, keepdims=True)
                sums[right, :, cut] = sums[right, :, cut] + column if right in seen else column
            totals[left] = totals[left] + rows if left in seen else rows
            seen.add(left)
        seen.add(right)

    ready, seen = set(), set()
    for only, left, *right_slots in jobs:

        def work(fresh):
            for slot in fresh:
                prepare(slot)
            for right in right_slots:
                pair(left, right, seen)

        fresh = [slot for slot in (left, *right_slots) if slot not in ready]
        ready.update(fresh)
        if only is None:
            work(fresh)
        else:
            pl.when(variant == only)(functools.partial(work, fresh))

    for which in (0, 1):

        @pl.when(variant == which)
        def _(which=which):
            for part in outs:
                found = [slot for slot, other in parts_of[which].items() if other == part]
                terms = [as_row(totals[i]) if i in lefts else sums[i] for i in found]
                results[part][...] = sum(terms, jnp.zeros((1, HALF), jnp.float32))


def pair_sums(flag, arrays, first_parts, second_parts, jobs):
    names = list(arrays)
    places = {}
    for name in names:
        if arrays[name].shape[0] == HALF:
            places[name] = (name, 0)
        else:
            places[name + "0"], places[name + "1"] = (name, 0), (name, HALF)
    parts_of = [
        {slot: part for slot, part in enumerate(parts) if part}
        for parts in (second_parts, first_parts)
    ]
    outs = sorted(set(parts_of[0].values()) | set(parts_of[1].values()))
    slots = len(first_parts)
    results = pl.pallas_call(
        functools.partial(pairs_kernel, parts_of, jobs, names, places, outs),
        out_shape=[jax.ShapeDtypeStruct((1, HALF), jnp.float32) for _ in outs],
        in_specs=[pl.BlockSpec(memory_space=pltpu.SMEM)]
        + [pl.BlockSpec(memory_space=pltpu.HBM)] * len(names),
        out_specs=[pl.BlockSpec(memory_space=pltpu.VMEM)] * len(outs),
        scratch_shapes=[
            pltpu.VMEM((slots, HALF, 1024), jnp.bfloat16),
            pltpu.VMEM((slots, HALF, LANES), jnp.float32),
            pltpu.VMEM((slots, 1, HALF), jnp.float32),
            pltpu.VMEM((slots, HALF, LANES), jnp.float32),
            pltpu.VMEM((slots, 1, HALF), jnp.float32),
            pltpu.SemaphoreType.DMA((slots,)),
        ],
        compiler_params=pltpu.CompilerParams(vmem_limit_bytes=32 * 1024 * 1024),
        cost_estimate=pl.CostEstimate(flops=1, bytes_accessed=1, transcendentals=0),
    )(flag, *[arrays[name] for name in names])
    return dict(zip(outs, results))


def whole(first_half, second_half):
    return jnp.concatenate([first_half[0], second_half[0]])


def after(value, *others):
    return lax.optimization_barrier((value, *others))[0]


def body(own):
    rows = own.shape[0]
    half = rows // 2
    first = lax.axis_index("gx") % 2 != lax.axis_index("gy") % 2

    gx, gy = lax.axis_index("gx"), lax.axis_index("gy")
    height, core = 2 * ((gy % 8) // 2) + gx % 2, gy % 2
    seam = ((height == 1) & (core == 1)) | ((height == 6) & (core == 0))
    flag = first.astype(jnp.int32).reshape(1)
    own_a = own[:half]
    own_b = lax.optimization_barrier(after(own, own_a)[half:])
    later = after(own, own_b)
    one_a = move(own_a, route(hop_one))
    one_b = move(own_b, route(hop_one))
    along = move(later, route(own_in_plane))
    across = move(later, route(own_across))
    two_a = move(one_a, route(hop_two))

    own_half = half_norms(own)
    diagonal = lax.broadcasted_iota(jnp.int32, (rows, rows), 0) == lax.broadcasted_iota(
        jnp.int32, (rows, rows), 1
    )
    same = jnp.where(diagonal, jnp.float32(0.0), kernel_block(own, own_half, own, own_half))
    total = jnp.sum(same, axis=1)
    two_b = move(after(one_b, total, own_half), route(hop_two))
    third_a, third_b = lax.optimization_barrier(
        (
            jnp.where(seam, along[:half], own[:half]),
            jnp.where(seam, along[half:], own[half:]),
        )
    )
    early = pair_sums(
        flag,
        dict(along=along, one_a=one_a, one_b=one_b),
        ["along0", "one_a", "one_b", "along1"],
        [None] * 4,
        [(1, 0, 1, 2), (1, 3, 1, 2)],
    )

    two_a_after = after(two_a, early)
    two_c_a = move(two_a_after, route(two_across))
    two_x_a = move(two_a_after, route(two_along_x))
    three_a = move(after(third_a, two_a), route(hop_three))
    three_b = move(after(third_b, two_b), route(hop_three))
    two_c_b = move(two_b, route(two_across))
    two_x_b = move(after(two_b, two_x_a), route(two_along_x))

    middle = pair_sums(
        flag,
        dict(own=own, across=after(across, three_a), two_a=two_a, two_b=two_b, two_c_a=two_c_a),
        ["own0", "across0", "across1", "own1", None],
        ["across0", "two_a", "two_b", "across1", "two_c_a"],
        [(None, 0, 1, 2), (None, 3, 1, 2), (0, 4, 1, 2)],
    )
    three_c_a = move(three_a, route(three_across))
    late = pair_sums(
        flag,
        dict(
            three_a=three_a, two_a=two_a, two_b=two_b, two_c_b=two_c_b, two_x_a=two_x_a,
            three_c_a=three_c_a,
        ),
        ["three_a", "two_a", "two_b", "three_c_a", None],
        ["three_a", "two_a", "two_b", "two_x_a", "two_c_b"],
        [(None, 0, 1, 2, 3), (0, 4, 1, 2)],
    )

    held = dict(route(own_in_plane))
    ahead = dict(route(hop_three))
    third = [(s, ahead[held[s] if is_seam(*PLACE[s]) else s]) for s in PLACE]
    over = dict(route(three_across))
    crossed = [(s, over[t]) for s, t in third if t in over]
    along_pairs = [p for p in route(own_in_plane) if is_first(*PLACE[p[1]])]
    one_pairs = [p for p in route(hop_one) if is_first(*PLACE[p[1]])]
    along_sums = move(whole(early["along0"], early["along1"]), back(along_pairs))
    across_sums = move(
        whole(middle["across0"], middle["across1"]), back(route(own_across))
    )

    three_b, _ = lax.optimization_barrier((three_b, (late, along_sums, across_sums)))
    three_c_b = move(three_b, route(three_across))
    last = pair_sums(
        flag,
        dict(
            three_b=three_b, two_a=two_a, two_b=two_b, two_x_a=two_x_a, two_x_b=two_x_b,
            three_a=three_a, three_c_a=three_c_a,
        ),
        ["three_b", "two_a", "two_b", "three_c_a", None, None],
        ["three_b", "two_a", "two_b", "two_x_a", "two_x_b", "three_a"],
        [(None, 0, 1, 2, 3), (0, 0, 4), (0, 5, 4)],
    )
    final = pair_sums(
        flag,
        dict(three_a=three_a, three_b=three_b, three_c_b=three_c_b),
        ["three_c_b", "three_a", "three_b"],
        [None] * 3,
        [(1, 0, 1, 2)],
    )

    total = total + whole(middle["own0"], middle["own1"])
    total = total + along_sums + across_sums
    total = total + move(
        after(
            whole(early["one_a"] + middle["two_c_a"], early["one_b"] + late["two_c_b"]), last
        ),
        back(one_pairs + route(hop_one, hop_two, two_across)),
    )
    total = total + move(
        whole(
            middle["two_a"] + late["two_a"] + last["two_a"],
            middle["two_b"] + late["two_b"] + last["two_b"],
        ),
        back(route(hop_one, hop_two)),
    )
    total = total + move(
        whole(
            late["three_a"] + last["three_a"] + final["three_a"],
            last["three_b"] + final["three_b"],
        ),
        back(third),
    )
    total = total + move(
        whole(
            late["two_x_a"] + last["two_x_a"] + late["three_c_a"] + last["three_c_a"],
            last["two_x_b"] + final["three_c_b"],
        ),
        back(crossed + route(hop_one, hop_two, two_along_x)),
    )
    return own_half + jnp.log(total)


PLACE = {number(*device): device for device in DEVICES}


def solution(mesh):
    in_specs = (P(AXES, None),)
    return jax.shard_map(
        body, mesh=mesh, in_specs=in_specs, out_specs=P(AXES), check_vma=False
    )
```

```python
import functools
import math

import jax
import jax.numpy as jnp
from jax import lax
from jax.experimental import pallas as pl
from jax.experimental.pallas import tpu as pltpu
from jax.sharding import PartitionSpec as P

BAND = 64
LOG2E = math.log2(math.e)
HALF = 512
TILE = 256
LANES = 128
AXES = ("gx", "gy")
NX, NY, NZ = 4, 4, 8

DEVICES = [
    (x, y, z, c) for x in range(NX) for y in range(NY) for z in range(NZ) for c in range(2)
]


def number(x, y, z, c):
    x, y, z = x % NX, y % NY, z % NZ
    return (2 * x + z % 2) * 32 + 8 * y + 2 * (z // 2) + c


def is_first(x, y, z, c):
    return c != z % 2


def hop_one(x, y, z, c):
    return (x, y, z + 1, c) if c else (x, y, z - 1, c)


def hop_two(x, y, z, c):
    if c:
        t = (z + 1) % NZ
        return (x, y - (t in (3, 5)), t, c)
    t = (z - 1) % NZ
    return (x, y + (t in (2, 4)), t, c)


def hop_three(x, y, z, c):
    return (x, y, z - 1, c) if c else (x, y, z + 1, c)


def is_seam(x, y, z, c):
    return (z, c) in ((1, 1), (6, 0))


def own_across(x, y, z, c):
    if not is_first(x, y, z, c):
        return (x, y, z, 1 - c)
    return (x, y + (z in (2, 4, 6)), z, 0) if c else (x, y - (z in (1, 3, 5)), z, 1)


def own_in_plane(x, y, z, c):
    if is_first(x, y, z, c):
        return (x - 1, y - (z == 0), z, c) if c else (x + 1, y + (z == 7), z, c)
    if is_seam(x, y, z, c):
        return (x, y - 1, z, c) if c else (x, y + 1, z, c)
    return None


def two_along_x(x, y, z, c):
    if is_first(x, y, z, c):
        return None
    return (x + 1, y + 1, z, c) if c else (x - 1, y - 1, z, c)


def two_across(x, y, z, c):
    if not is_first(x, y, z, c):
        return None
    return (x, y + 1, z, 0) if c else (x, y - 1, z, 1)


def three_across(x, y, z, c):
    if is_first(x, y, z, c):
        return None
    return (x, y, z, 1 - c)


def route(*hops):
    pairs = []
    for source in DEVICES:
        at = source
        for hop in hops:
            at = at and hop(*at)
            at = at and (at[0] % NX, at[1] % NY, at[2] % NZ, at[3])
        if at:
            pairs.append((number(*source), number(*at)))
    return pairs


def back(pairs):
    return [(target, source) for source, target in pairs]


def move(value, pairs):
    return lax.ppermute(value, AXES, pairs)


def half_norms(block):
    values = block.astype(jnp.float32)
    return jnp.sum(values * values, axis=1) / (2.0 * BAND)


def kernel_block(left, left_half, right, right_half):
    inner = lax.dot_general(
        left, right, (((1,), (1,)), ((), ())), preferred_element_type=jnp.float32
    )
    return jnp.exp(inner / BAND - left_half[:, None] - right_half[None, :])


def lane_sums(values):
    return functools.reduce(
        lambda x, y: x + y,
        [values[:, i : i + LANES] for i in range(0, values.shape[1], LANES)],
    )


def as_row(partial):
    return jnp.sum(jnp.transpose(partial), axis=0, keepdims=True)


def pairs_kernel(parts_of, jobs, names, places, outs, flag, *refs):
    sources = dict(zip(names, refs[: len(names)]))
    results = dict(zip(outs, refs[len(names) : len(names) + len(outs)]))
    blocks, norms, rights, totals, sums, sems = refs[len(names) + len(outs) :]
    variant = flag[0]
    lefts = {job[1] for job in jobs}

    for which in (0, 1):

        @pl.when(variant == which)
        def _(which=which):
            for slot, part in parts_of[which].items():
                name, offset = places[part]
                pltpu.make_async_copy(
                    sources[name].at[pl.ds(offset, HALF)], blocks.at[slot], sems.at[slot]
                ).start()

    def prepare(slot):
        pltpu.make_async_copy(blocks.at[slot], blocks.at[slot], sems.at[slot]).wait()
        values = blocks[slot].astype(jnp.float32)
        squares = lane_sums(values * values) * (LOG2E / (2.0 * BAND))
        if slot in lefts:
            norms[slot] = jnp.broadcast_to(
                jnp.sum(squares, axis=1, keepdims=True), (HALF, LANES)
            )
        else:
            rights[slot] = as_row(squares)

    def pair(left, right, seen):
        for at in range(0, HALF, TILE):
            inner = lax.dot_general(
                blocks[left],
                blocks[right, at : at + TILE],
                (((1,), (1,)), ((), ())),
                preferred_element_type=jnp.float32,
            )
            rows = None
            for lane in range(0, TILE, LANES):
                cut = slice(at + lane, at + lane + LANES)
                value = jnp.exp2(
                    inner[:, lane : lane + LANES] * (LOG2E / BAND)
                    - norms[left]
                    - rights[right, :, cut]
                )
                rows = value if rows is None else rows + value
                column = jnp.sum(value, axis=0, keepdims=True)
                sums[right, :, cut] = sums[right, :, cut] + column if right in seen else column
            totals[left] = totals[left] + rows if left in seen else rows
            seen.add(left)
        seen.add(right)

    ready, seen = set(), set()
    for only, left, *right_slots in jobs:

        def work(fresh):
            for slot in fresh:
                prepare(slot)
            for right in right_slots:
                pair(left, right, seen)

        fresh = [slot for slot in (left, *right_slots) if slot not in ready]
        ready.update(fresh)
        if only is None:
            work(fresh)
        else:
            pl.when(variant == only)(functools.partial(work, fresh))

    for which in (0, 1):

        @pl.when(variant == which)
        def _(which=which):
            for part in outs:
                found = [slot for slot, other in parts_of[which].items() if other == part]
                terms = [as_row(totals[i]) if i in lefts else sums[i] for i in found]
                results[part][...] = sum(terms, jnp.zeros((1, HALF), jnp.float32))


def pair_sums(flag, arrays, first_parts, second_parts, jobs):
    names = list(arrays)
    places = {}
    for name in names:
        if arrays[name].shape[0] == HALF:
            places[name] = (name, 0)
        else:
            places[name + "0"], places[name + "1"] = (name, 0), (name, HALF)
    parts_of = [
        {slot: part for slot, part in enumerate(parts) if part}
        for parts in (second_parts, first_parts)
    ]
    outs = sorted(set(parts_of[0].values()) | set(parts_of[1].values()))
    slots = len(first_parts)
    results = pl.pallas_call(
        functools.partial(pairs_kernel, parts_of, jobs, names, places, outs),
        out_shape=[jax.ShapeDtypeStruct((1, HALF), jnp.float32) for _ in outs],
        in_specs=[pl.BlockSpec(memory_space=pltpu.SMEM)]
        + [pl.BlockSpec(memory_space=pltpu.HBM)] * len(names),
        out_specs=[pl.BlockSpec(memory_space=pltpu.VMEM)] * len(outs),
        scratch_shapes=[
            pltpu.VMEM((slots, HALF, 1024), jnp.bfloat16),
            pltpu.VMEM((slots, HALF, LANES), jnp.float32),
            pltpu.VMEM((slots, 1, HALF), jnp.float32),
            pltpu.VMEM((slots, HALF, LANES), jnp.float32),
            pltpu.VMEM((slots, 1, HALF), jnp.float32),
            pltpu.SemaphoreType.DMA((slots,)),
        ],
        compiler_params=pltpu.CompilerParams(vmem_limit_bytes=32 * 1024 * 1024),
        cost_estimate=pl.CostEstimate(flops=1, bytes_accessed=1, transcendentals=0),
    )(flag, *[arrays[name] for name in names])
    return dict(zip(outs, results))


def whole(first_half, second_half):
    return jnp.concatenate([first_half[0], second_half[0]])


def after(value, *others):
    return lax.optimization_barrier((value, *others))[0]


def body(own):
    rows = own.shape[0]
    half = rows // 2
    first = lax.axis_index("gx") % 2 != lax.axis_index("gy") % 2

    gx, gy = lax.axis_index("gx"), lax.axis_index("gy")
    height, core = 2 * ((gy % 8) // 2) + gx % 2, gy % 2
    seam = ((height == 1) & (core == 1)) | ((height == 6) & (core == 0))
    flag = first.astype(jnp.int32).reshape(1)
    own_a = own[:half]
    own_b = lax.optimization_barrier(after(own, own_a)[half:])
    later = after(own, own_b)
    one_a = move(own_a, route(hop_one))
    one_b = move(own_b, route(hop_one))
    along = move(later, route(own_in_plane))
    across = move(later, route(own_across))
    two_a = move(one_a, route(hop_two))

    own_half = half_norms(own)
    diagonal = lax.broadcasted_iota(jnp.int32, (rows, rows), 0) == lax.broadcasted_iota(
        jnp.int32, (rows, rows), 1
    )
    same = jnp.where(diagonal, jnp.float32(0.0), kernel_block(own, own_half, own, own_half))
    total = jnp.sum(same, axis=1)
    two_b = move(after(one_b, total, own_half), route(hop_two))
    third_a, third_b = lax.optimization_barrier(
        (
            jnp.where(seam, along[:half], own[:half]),
            jnp.where(seam, along[half:], own[half:]),
        )
    )
    early = pair_sums(
        flag,
        dict(along=along, one_a=one_a, one_b=one_b),
        ["along0", "one_a", "one_b", "along1"],
        [None] * 4,
        [(1, 0, 1, 2), (1, 3, 1, 2)],
    )

    two_a_after = after(two_a, early)
    two_c_a = move(two_a_after, route(two_across))
    two_x_a = move(two_a_after, route(two_along_x))
    three_a = move(after(third_a, two_a), route(hop_three))
    three_b = move(after(third_b, two_b), route(hop_three))
    two_c_b = move(two_b, route(two_across))
    two_x_b = move(after(two_b, two_x_a), route(two_along_x))

    middle = pair_sums(
        flag,
        dict(own=own, across=after(across, three_a), two_a=two_a, two_b=two_b, two_c_a=two_c_a),
        ["own0", "across0", "across1", "own1", None],
        ["across0", "two_a", "two_b", "across1", "two_c_a"],
        [(None, 0, 1, 2), (None, 3, 1, 2), (0, 4, 1, 2)],
    )
    three_c_a = move(three_a, route(three_across))
    late = pair_sums(
        flag,
        dict(
            three_a=three_a, two_a=two_a, two_b=two_b, two_c_b=two_c_b, two_x_a=two_x_a,
            three_c_a=three_c_a,
        ),
        ["three_a", "two_a", "two_b", "three_c_a", None],
        ["three_a", "two_a", "two_b", "two_x_a", "two_c_b"],
        [(None, 0, 1, 2, 3), (0, 4, 1, 2)],
    )

    held = dict(route(own_in_plane))
    ahead = dict(route(hop_three))
    third = [(s, ahead[held[s] if is_seam(*PLACE[s]) else s]) for s in PLACE]
    over = dict(route(three_across))
    crossed = [(s, over[t]) for s, t in third if t in over]
    along_pairs = [p for p in route(own_in_plane) if is_first(*PLACE[p[1]])]
    one_pairs = [p for p in route(hop_one) if is_first(*PLACE[p[1]])]
    along_sums = move(whole(early["along0"], early["along1"]), back(along_pairs))
    across_sums = move(
        whole(middle["across0"], middle["across1"]), back(route(own_across))
    )

    three_b, _ = lax.optimization_barrier((three_b, (late, along_sums, across_sums)))
    three_c_b = move(three_b, route(three_across))
    last = pair_sums(
        flag,
        dict(
            three_b=three_b, two_a=two_a, two_b=two_b, two_x_a=two_x_a, two_x_b=two_x_b,
            three_a=three_a, three_c_a=three_c_a,
        ),
        ["three_b", "two_a", "two_b", "three_c_a", None, None],
        ["three_b", "two_a", "two_b", "two_x_a", "two_x_b", "three_a"],
        [(None, 0, 1, 2, 3), (0, 0, 4), (0, 5, 4)],
    )
    final = pair_sums(
        flag,
        dict(three_a=three_a, three_b=three_b, three_c_b=three_c_b),
        ["three_c_b", "three_a", "three_b"],
        [None] * 3,
        [(1, 0, 1, 2)],
    )

    total = total + whole(middle["own0"], middle["own1"])
    total = total + along_sums + across_sums
    total = total + move(
        whole(early["one_a"] + middle["two_c_a"], early["one_b"] + late["two_c_b"]),
        back(one_pairs + route(hop_one, hop_two, two_across)),
    )
    total = total + move(
        whole(
            middle["two_a"] + late["two_a"] + last["two_a"],
            middle["two_b"] + late["two_b"] + last["two_b"],
        ),
        back(route(hop_one, hop_two)),
    )
    total = total + move(
        whole(
            late["three_a"] + last["three_a"] + final["three_a"],
            last["three_b"] + final["three_b"],
        ),
        back(third),
    )
    total = total + move(
        whole(
            late["two_x_a"] + last["two_x_a"] + late["three_c_a"] + last["three_c_a"],
            last["two_x_b"] + final["three_c_b"],
        ),
        back(crossed + route(hop_one, hop_two, two_along_x)),
    )
    return own_half + jnp.log(total)


PLACE = {number(*device): device for device in DEVICES}


def solution(mesh):
    in_specs = (P(AXES, None),)
    return jax.shard_map(
        body, mesh=mesh, in_specs=in_specs, out_specs=P(AXES), check_vma=False
    )
```
